32 devices in a mesh: shard: 4 (over x, core), replica: 8 (over z, y).
Axes of the slice: x: 2, y: 2, z: 4, core: 2. Of those that a mesh axis runs over, the one named last changes fastest.
Arguments:
- tokens: bfloat16 [10240, 1024], P(('shard', 'replica')), may hold values from -6 to 6
- qkv_weight: bfloat16 [1024, 3072], P('shard'), may hold values from -0.1875 to 0.1875
- query_bias: bfloat16 [1024], P('shard'), may hold values from -3 to 3
- value_bias: bfloat16 [1024], P('shard'), may hold values from -3 to 3
- proj_weight: bfloat16 [1024, 1024], P('shard'), may hold values from -0.75 to 0.75
- proj_bias: bfloat16 [1024], P('shard'), may hold values from -3 to 3
- attn_gain: bfloat16 [1024], P('shard'), may hold values from 0.5 to 1.5
- attn_shift: bfloat16 [1024], P('shard'), may hold values from -3 to 3
- inner_weight: bfloat16 [1024, 4096], P('shard'), may hold values from -0.1875 to 0.1875
- inner_bias: bfloat16 [4096], P('shard'), may hold values from -3 to 3
- outer_weight: bfloat16 [4096, 1024], P('shard'), may hold values from -0.09375 to 0.09375
- outer_bias: bfloat16 [1024], P('shard'), may hold values from -3 to 3
- ffn_gain: bfloat16 [1024], P('shard'), may hold values from 0.5 to 1.5
- ffn_shift: bfloat16 [1024], P('shard'), may hold values from -3 to 3
- cotangent: bfloat16 [10240, 1024], P(('shard', 'replica')), may hold values from -6 to 6
Outputs:
- result: float32 [10240, 1024], P(('shard', 'replica'))
- input_grad: float32 [10240, 1024], P(('shard', 'replica'))
- grad_qkv: float32 [1024, 3072], P('shard')
- grad_qbias: float32 [1024], P('shard')
- grad_vbias: float32 [1024], P('shard')
- grad_proj: float32 [1024, 1024], P('shard')
- grad_pbias: float32 [1024], P('shard')
- grad_again: float32 [1024], P('shard')
- grad_ashift: float32 [1024], P('shard')
- grad_inner: float32 [1024, 4096], P('shard')
- grad_ibias: float32 [4096], P('shard')
- grad_outer: float32 [4096, 1024], P('shard')
- grad_obias: float32 [1024], P('shard')
- grad_fgain: float32 [1024], P('shard')
- grad_fshift: float32 [1024], P('shard')
The draws below stay inside these ranges and needn't reach their ends.
All inputs are finite; a program needn't handle non-finite values.
Results may differ from the reference program's by a relative error of at most 0.02.
Values may be sent and summed in bfloat16 or wider, within the bound.
No kernel may reach another device: no remote copies, remote signals or barrier semaphores. Data moves between devices by JAX's collectives and lax.ppermute only.
A program may use at most 192 MiB of HBM per device.

```python
import math
import jax
import jax.numpy as jnp
from jax import lax

D = 1024
FF = 4096
HEADS = 16
HEAD = 64
SEQ_LEN = 320
TOKENS = 10240


def block_levels(stream_key, shape, shards, low, top_value):
    factor_of, own = 1.0, jax.random.fold_in(stream_key, 6)
    for dim, shards_of in shards:
        draws = jnp.exp(jax.random.uniform(jax.random.fold_in(own, dim), (shards_of,), jnp.float32, low / len(shards), top_value / len(shards)))
        factor_of = factor_of * jnp.repeat(draws, shape[dim] // shards_of).reshape([-1 if axis == dim else 1 for axis in range(len(shape))])
    return factor_of


def bell_draw(own_key, dims, deviation, bound, pieces=(), kind=jnp.bfloat16):
    values = jax.random.normal(own_key, dims, jnp.float32) * deviation
    if len(pieces) > 0:
        values = block_levels(own_key, dims, pieces, -0.22, 0.18) * values
    return jnp.clip(values, min=-bound, max=bound).astype(kind)


def setup_inputs(seed: int = 0) -> dict:
    seeds = jax.random.split(jax.random.key(seed), 16)
    tokens = bell_draw(seeds[0], (TOKENS, D), 1.0, 6.0, ((0, 32),))
    qkv_weight = bell_draw(seeds[1], (D, 3 * D), D ** -0.5, 0.1875, ((0, 4),))
    query_bias = bell_draw(seeds[2], (D,), 0.5, 3.0, ((0, 4),))
    value_bias = bell_draw(seeds[3], (D,), 0.5, 3.0, ((0, 4),))
    proj_weight = bell_draw(seeds[4], (D, D), (D // 16) ** -0.5, 0.75, ((0, 4),))
    proj_bias = bell_draw(seeds[5], (D,), 0.5, 3.0, ((0, 4),))
    attn_gain = jnp.clip(1.0 + 0.1 * jax.random.normal(seeds[6], (D,), jnp.float32), 0.5, 1.5).astype(jnp.bfloat16)
    attn_shift = bell_draw(seeds[7], (D,), 0.5, 3.0, ((0, 4),))
    inner_weight = bell_draw(seeds[8], (D, FF), D ** -0.5, 0.1875, ((0, 4),))
    inner_bias = bell_draw(seeds[9], (FF,), 0.5, 3.0, ((0, 4),))
    outer_weight = bell_draw(seeds[10], (FF, D), FF ** -0.5, 0.09375, ((0, 4),))
    outer_bias = bell_draw(seeds[11], (D,), 0.5, 3.0, ((0, 4),))
    ffn_gain = jnp.clip(1.0 + 0.1 * jax.random.normal(seeds[12], (D,), jnp.float32), 0.5, 1.5).astype(jnp.bfloat16)
    ffn_shift = bell_draw(seeds[13], (D,), 0.5, 3.0, ((0, 4),))
    cotangent = bell_draw(seeds[14], (TOKENS, D), 1.0, 6.0, ((0, 32),))
    return dict(tokens=tokens, qkv_weight=qkv_weight, query_bias=query_bias, value_bias=value_bias, proj_weight=proj_weight, proj_bias=proj_bias, attn_gain=attn_gain, attn_shift=attn_shift, inner_weight=inner_weight, inner_bias=inner_bias, outer_weight=outer_weight, outer_bias=outer_bias, ffn_gain=ffn_gain, ffn_shift=ffn_shift, cotangent=cotangent)


@jax.custom_vjp
def low(v):
    return lax.optimization_barrier(v.astype(jnp.bfloat16)).astype(jnp.float32)

@jax.custom_vjp
def low_back(v):
    return v

def low_keep(v):
    return (low(v), None)

def low_pass(kept, grad):
    return (grad,)

def back_keep(v):
    return (v, None)

def back_low(kept, grad):
    return (low(grad),)
low.defvjp(low_keep, low_pass)
low_back.defvjp(back_keep, back_low)
epsilon = 1e-05
highest = lax.Precision.HIGHEST

def matmul(former, latter):
    return jnp.dot(former, latter, precision=highest, preferred_element_type=jnp.float32)

def normalize(activation, scaling, offset):
    centred = activation - lax.optimization_barrier(jnp.mean(activation, axis=-1, keepdims=True))
    spread = lax.optimization_barrier(jnp.mean(centred * centred, axis=-1, keepdims=True))
    return centred * lax.rsqrt(spread + epsilon) * scaling + offset

def layer(inputs, qkv_weight, query_bias, value_bias, proj_weight, proj_bias, attn_gain, attn_shift, inner_weight, inner_bias, outer_weight, outer_bias, ffn_gain, ffn_shift):
    sequences = inputs.shape[0] // SEQ_LEN
    projected = matmul(inputs, qkv_weight)
    queries = low(low_back(projected[:, :D] + query_bias))
    key_rows = low(low_back(projected[:, D:2 * D]))
    values = low(low_back(projected[:, 2 * D:] + value_bias))
    head_shape = (sequences, SEQ_LEN, HEADS, HEAD)
    scores = jnp.einsum('bqhd,bkhd->bhqk', queries.reshape(head_shape), key_rows.reshape(head_shape), precision=highest) * HEAD ** (-0.5)
    attend = low(jax.nn.softmax(low_back(scores), axis=-1))
    context = jnp.einsum('bhqk,bkhd->bqhd', attend, values.reshape(head_shape), precision=highest)
    context = low(low_back(context.reshape(-1, D)))
    branch = low_back(matmul(context, proj_weight) + proj_bias)
    hidden_one = normalize(inputs + branch, attn_gain, attn_shift)
    inner_pre = low_back(matmul(low(hidden_one), inner_weight) + inner_bias)
    active = low(jax.nn.gelu(inner_pre, approximate=False))
    outer_out = low_back(matmul(active, outer_weight) + outer_bias)
    return normalize(hidden_one + outer_out, ffn_gain, ffn_shift)

def reference(tokens, qkv_weight, query_bias, value_bias, proj_weight, proj_bias, attn_gain, attn_shift, inner_weight, inner_bias, outer_weight, outer_bias, ffn_gain, ffn_shift, cotangent):
    params = tuple((member.astype(jnp.float32) for member in (qkv_weight, query_bias, value_bias, proj_weight, proj_bias, attn_gain, attn_shift, inner_weight, inner_bias, outer_weight, outer_bias, ffn_gain, ffn_shift)))
    sequences = TOKENS // SEQ_LEN
    grouped = math.gcd(sequences, max(1, 4096 // SEQ_LEN))
    blocks = sequences // grouped
    inputs = tokens.astype(jnp.float32).reshape(blocks, grouped * SEQ_LEN, D)
    upstream = cotangent.astype(jnp.float32).reshape(blocks, grouped * SEQ_LEN, D)

    def advance(totals, couple):
        result, backward = jax.vjp(layer, couple[0], *params)
        gradients = backward(couple[1])
        return (tuple((t + g for t, g in zip(totals, gradients[1:]))), (result, gradients[0]))
    initial = tuple((jnp.zeros_like(member) for member in params))
    totals, (results, input_grads) = lax.scan(advance, initial, (inputs, upstream))
    grad_qkv, grad_qbias, grad_vbias, grad_proj, grad_pbias, grad_again, grad_ashift, grad_inner, grad_ibias, grad_outer, grad_obias, grad_fgain, grad_fshift = totals
    return (results.reshape(TOKENS, D), input_grads.reshape(TOKENS, D), grad_qkv, grad_qbias, grad_vbias, grad_proj, grad_pbias, grad_again, grad_ashift, grad_inner, grad_ibias, grad_outer, grad_obias, grad_fgain, grad_fshift)
```

```python
import jax
import jax.numpy as jnp
from jax import lax
from jax.sharding import PartitionSpec as P

HEAD = 64
EPS = 1e-05
AXES = ("shard", "replica")
F32 = jnp.float32
BF16 = jnp.bfloat16


def tdot(former, latter):
    return lax.dot_general(
        former, latter, (((0,), (0,)), ((), ())), preferred_element_type=F32
    )


def ndot(former, latter):
    return lax.dot_general(
        former, latter, (((1,), (1,)), ((), ())), preferred_element_type=F32
    )


def mdot(former, latter):
    return jnp.dot(former, latter, preferred_element_type=F32)


def column_sums(matrix):
    return jnp.sum(matrix.astype(F32), axis=0)


def after(value, *others):
    return lax.optimization_barrier((value,) + others)[0]


def make(shards, replicas):
    bits = []
    bit = 1
    while bit < replicas:
        bits.append(bit)
        bit *= 2

    def swap(array, shard_bit, replica_bit):
        pairs = [
            (s * replicas + r, (s ^ shard_bit) * replicas + (r ^ replica_bit))
            for s in range(shards)
            for r in range(replicas)
        ]
        return lax.ppermute(array, AXES, pairs)

    def across(array):
        return swap(array, 2, 0)

    def core(array):
        return swap(array, 1, 0)

    def rows(array, start, count):
        return lax.dynamic_slice_in_dim(array, start, count, axis=0)

    def put(whole, part, start):
        return lax.dynamic_update_slice_in_dim(whole, part, start, axis=0)

    def per_device(
        tokens,
        qkv_weight,
        query_bias,
        value_bias,
        proj_weight,
        proj_bias,
        attn_gain,
        attn_shift,
        inner_weight,
        inner_bias,
        outer_weight,
        outer_bias,
        ffn_gain,
        ffn_shift,
        cotangent,
    ):
        s = lax.axis_index("shard")
        r = lax.axis_index("replica")
        xbit = s // 2
        cbit = s % 2
        ybit = r % 2
        zbit = (r // 2) % 2
        length, width = tokens.shape

        def place(own, near, far, diag):
            count = own.shape[0]
            whole = jnp.zeros((shards * count,) + own.shape[1:], own.dtype)
            whole = put(whole, own, s * count)
            whole = put(whole, near, (s ^ 1) * count)
            whole = put(whole, far, (s ^ 2) * count)
            return put(whole, diag, (s ^ 3) * count)

        small = (
            query_bias,
            value_bias,
            proj_bias,
            attn_gain,
            attn_shift,
            inner_bias,
            outer_bias,
            ffn_gain,
            ffn_shift,
        )
        pack = jnp.concatenate(small)
        far_pack = across(pack)
        both = core(jnp.stack([pack, far_pack]))
        packs = place(pack[None], both[:1], far_pack[None], both[1:]).astype(F32)
        vectors = []
        offset = 0
        for member in small:
            count = member.shape[0]
            vectors.append(packs[:, offset : offset + count].reshape(-1))
            offset += count
        qbias, vbias, pbias, again, ashift, ibias, obias, fgain, fshift = vectors

        parity = ybit ^ zbit

        def gather_two(own, gate):
            count = own.shape[0]
            near = core(own)
            half, quarter = count // 2, count // 4
            first = rows(own, parity * half, half)
            if gate is not None:
                first = after(first, gate)
            first = across(first)
            from_y = swap(first[:quarter], 0, 1)
            from_z = swap(first[quarter:], 0, 2)
            far = jnp.zeros_like(own)
            far = put(far, first, parity * half)
            far = put(far, from_y, (1 - parity) * half)
            far = put(far, from_z, (1 - parity) * half + quarter)
            return place(own, near, far, core(far)), first

        mine = ybit + 2 * zbit

        def gather_four(own, gate):
            count = own.shape[0]
            near = core(own)
            quarter, eighth = count // 4, count // 8
            first = rows(own, mine * quarter, quarter)
            if gate is not None:
                first = after(first, gate)
            first = across(first)
            from_y = swap(first, 0, 1)
            from_z = swap(first, 0, 2)
            diag_y = swap(from_z[:eighth], 0, 1)
            diag_z = swap(from_y[eighth:], 0, 2)
            far = jnp.zeros_like(own)
            far = put(far, first, mine * quarter)
            far = put(far, from_y, (mine ^ 1) * quarter)
            far = put(far, from_z, (mine ^ 2) * quarter)
            far = put(far, diag_y, (mine ^ 3) * quarter)
            far = put(far, diag_z, (mine ^ 3) * quarter + eighth)
            return place(own, near, far, core(far)), first

        qkv, gate = gather_two(qkv_weight, None)
        proj, gate = gather_two(proj_weight, gate)
        inner, gate = gather_four(inner_weight, gate)
        outer, gate = gather_four(outer_weight, gate)

        def pick(array, which):
            split = array.reshape(array.shape[0], 2, 2, array.shape[1] // 4)
            part = lax.dynamic_slice_in_dim(split, which, 1, axis=2)
            return part[:, :, 0, :]

        def column(part, which):
            return lax.dynamic_slice_in_dim(part, which, 1, axis=1)[:, 0, :]

        def add(a, b):
            return (a.astype(F32) + b.astype(F32)).astype(BF16)

        def reduce_rows(send, keep):
            got = across(send)
            here = None
            chain = []
            for bit in bits:
                half = keep.shape[0] // 2
                flag = (r // bit) % 2
                going = add(rows(keep, (1 - flag) * half, half), rows(got, (1 - flag) * half, half))
                staying = add(rows(keep, flag * half, half), rows(got, flag * half, half))
                got = swap(going, 0, bit)
                keep = staying
                chain.append((bit, flag))
            here = add(keep, got)
            for bit, flag in reversed(chain):
                other = swap(here, 0, bit)
                here = jnp.where(
                    flag == 1,
                    jnp.concatenate([other, here]),
                    jnp.concatenate([here, other]),
                )
            return here.astype(F32)

        def weight_grad(x_own, x_got, g_own, g_got):
            def part(which):
                return (
                    tdot(column(x_own, which), g_own) + tdot(column(x_got, which), g_got)
                ).astype(BF16)

            return reduce_rows(part(1 - xbit), part(xbit))

        head_count = width // HEAD
        score_scale = HEAD ** (-0.5)
        inputs = tokens.astype(F32)
        projected = mdot(tokens, qkv)
        queries = (projected[:, :width] + qbias).astype(BF16)
        key_rows = projected[:, width : 2 * width].astype(BF16)
        values = (projected[:, 2 * width :] + vbias).astype(BF16)
        query_heads = queries.reshape(length, head_count, HEAD)
        key_heads = key_rows.reshape(length, head_count, HEAD)
        value_heads = values.reshape(length, head_count, HEAD)

        def score_block():
            return (
                jnp.einsum("qhd,khd->hqk", query_heads, key_heads, preferred_element_type=F32)
                * score_scale
            )

        scores = score_block()
        logsum = jax.nn.logsumexp(scores, axis=-1, keepdims=True)
        attend = jnp.exp(scores - logsum)
        attend_low = attend.astype(BF16)
        context = jnp.einsum("hqk,khd->qhd", attend_low, value_heads, preferred_element_type=F32)
        context = context.reshape(length, width).astype(BF16)
        tokens_got = core(pick(tokens, 1 - cbit))
        context_got = core(pick(context, 1 - cbit))

        def norm(total):
            centred = total - jnp.mean(total, axis=-1, keepdims=True)
            inverse = lax.rsqrt(jnp.mean(centred * centred, axis=-1, keepdims=True) + EPS)
            return centred * inverse, inverse

        def norm_back(upstream, normal, inverse, gain):
            scaled = upstream * gain
            grad = inverse * (
                scaled
                - jnp.mean(scaled, axis=-1, keepdims=True)
                - normal * jnp.mean(scaled * normal, axis=-1, keepdims=True)
            )
            return grad, jnp.sum(upstream * normal, axis=0), jnp.sum(upstream, axis=0)

        first_sum = inputs + (mdot(context, proj) + pbias)
        normal_one, inverse_one = norm(first_sum)
        hidden_one = normal_one * again + ashift
        hidden_low = hidden_one.astype(BF16)
        hidden_got = core(pick(hidden_low, 1 - cbit))
        inner_pre = mdot(hidden_low, inner) + ibias
        phi_big = 0.5 * (1.0 + lax.erf(inner_pre * (0.5**0.5)))
        slope = phi_big + inner_pre * jnp.exp(-0.5 * inner_pre * inner_pre) * (0.15915494309189535**0.5)
        active = (inner_pre * phi_big).astype(BF16)
        slope = slope.astype(BF16)
        active_got = core(pick(active, 1 - cbit))
        second_sum = hidden_one + (mdot(active, outer) + obias)
        normal_two, inverse_two = norm(second_sum)
        result = normal_two * fgain + fshift

        second_grad, grad_fgain, grad_fshift = norm_back(
            cotangent.astype(F32), normal_two, inverse_two, fgain
        )
        outer_grad = second_grad.astype(BF16)
        outer_grad_got = core(outer_grad)
        grad_outer = weight_grad(pick(active, cbit), active_got, outer_grad, outer_grad_got)
        grad_obias = column_sums(outer_grad)
        inner_grad = (ndot(outer_grad, outer) * slope.astype(F32)).astype(BF16)
        inner_grad_got = core(inner_grad)
        grad_inner = weight_grad(pick(hidden_low, cbit), hidden_got, inner_grad, inner_grad_got)
        grad_ibias = column_sums(inner_grad)
        hidden_grad = second_grad + ndot(inner_grad, inner)
        first_grad, grad_again, grad_ashift = norm_back(hidden_grad, normal_one, inverse_one, again)
        branch_grad = first_grad.astype(BF16)
        branch_grad_got = core(branch_grad)
        grad_proj = weight_grad(pick(context, cbit), context_got, branch_grad, branch_grad_got)
        grad_pbias = column_sums(branch_grad)
        context_grad = ndot(branch_grad, proj).astype(BF16).reshape(length, head_count, HEAD)
        attend_again = jnp.exp(score_block() - logsum)
        attend_grad = jnp.einsum("qhd,khd->hqk", context_grad, value_heads, preferred_element_type=F32)
        value_grad = jnp.einsum(
            "hqk,qhd->khd", attend_again.astype(BF16), context_grad, preferred_element_type=F32
        )
        score_grad = attend_again * (
            attend_grad - jnp.sum(attend_grad * attend_again, axis=-1, keepdims=True)
        )
        score_grad = score_grad.astype(BF16)
        query_grad = (
            jnp.einsum("hqk,khd->qhd", score_grad, key_heads, preferred_element_type=F32) * score_scale
        )
        key_grad = (
            jnp.einsum("hqk,qhd->khd", score_grad, query_heads, preferred_element_type=F32)
            * score_scale
        )
        query_low = query_grad.reshape(length, width).astype(BF16)
        key_low = key_grad.reshape(length, width).astype(BF16)
        value_low = value_grad.reshape(length, width).astype(BF16)
        mixed_grad = jnp.concatenate([query_low, key_low, value_low], axis=1)
        mixed_got = core(mixed_grad)
        grad_qkv = weight_grad(pick(tokens, cbit), tokens_got, mixed_grad, mixed_got)
        grad_qbias = column_sums(query_low)
        grad_vbias = column_sums(value_low)
        input_grad = first_grad + ndot(mixed_grad, qkv)

        little = (
            grad_qbias,
            grad_vbias,
            grad_pbias,
            grad_again,
            grad_ashift,
            grad_ibias,
            grad_obias,
            grad_fgain,
            grad_fshift,
        )
        packed = jnp.concatenate([member.reshape(shards, -1) for member in little], axis=1)
        packed = packed + core(packed)
        packed = rows(packed, xbit * 2, 2) + across(rows(packed, (1 - xbit) * 2, 2))
        for bit in bits:
            packed = packed + swap(packed, 0, bit)
        packed = rows(packed, cbit, 1)[0]
        summed = []
        offset = 0
        for member in little:
            count = member.shape[0] // shards
            summed.append(packed[offset : offset + count])
            offset += count
        (
            grad_qbias,
            grad_vbias,
            grad_pbias,
            grad_again,
            grad_ashift,
            grad_ibias,
            grad_obias,
            grad_fgain,
            grad_fshift,
        ) = summed
        return (
            result,
            input_grad,
            grad_qkv,
            grad_qbias,
            grad_vbias,
            grad_proj,
            grad_pbias,
            grad_again,
            grad_ashift,
            grad_inner,
            grad_ibias,
            grad_outer,
            grad_obias,
            grad_fgain,
            grad_fshift,
        )

    return per_device


def solution(mesh):
    both = P(("shard", "replica"), None)
    rows = P("shard", None)
    vec = P("shard")
    return jax.shard_map(
        make(mesh.shape["shard"], mesh.shape["replica"]),
        mesh=mesh,
        in_specs=(both, rows, vec, vec, rows, vec, vec, vec, rows, vec, rows, vec, vec, vec, both),
        out_specs=(both, both, rows, vec, vec, rows, vec, vec, vec, rows, vec, rows, vec, vec, vec),
        check_vma=False,
    )
```
